256 devices in a mesh: tm: 8 (over z_hi, y), row: 8 (over z_lo, core), blk: 4 (over x).
Axes of the slice: x: 4, y: 4, z: 8 (z_hi: 2, z_lo: 4; z = z_hi * 4 + z_lo), core: 2. Of those that a mesh axis runs over, the one named last changes fastest.
Arguments:
- right_side: float32 [32, 32, 16, 8, 384], P('tm', None, 'row', 'blk'), may hold values from -16 to 16
- stiffness: bfloat16 [16, 8, 10, 384, 384], P('row', 'blk'), may hold values from -0.039794922 to 0.039794922
- segments: int32 [16, 8, 10], P('row', 'blk'), may hold values from 1 to 4
- connectivity: int32 [16, 8, 10, 2], P('row', 'blk'), may hold values from 0 to 15, as said below
- lumped_mass: float32 [16, 8, 384], P('row', 'blk'), may hold values from 0.25 to 4
- stiff_diag: float32 [16, 8, 384], P('row', 'blk'), may hold values from 1.5 to 16
Outputs:
- correction: float32 [32, 32, 16, 8, 384], P('tm', None, 'row', 'blk')
The draws below stay inside these ranges and needn't reach their ends.
Inputs may be any that keep to these rules, and one draw needn't show every extreme that they name: `connectivity`: every named block column lies at most 2 lattice sites from its block row along each lattice dimension, counted around the lattice (the lattice closes on itself in both dimensions).
All inputs are finite; a program needn't handle non-finite values.
Results may differ from the reference program's by a relative error of at most 0.0003.
Values may be sent and summed in bfloat16 or wider, within the bound.
A program may use at most 128 MiB of HBM per device.

```python
import math
import jax
import jax.numpy as jnp
from jax import lax

STEPS = 32
BLOCK = 384
LINKS = 10
SWEEPS = 2
CASES = 32
SIDE = 2
LR = 16
LB = 8


def draw_connectivity(key, part):
    key = jax.random.fold_in(key, 11)
    key_rows, key_cols = jax.random.split(key)
    row_offsets = jax.random.randint(key_rows, (LR, LB, LINKS), -SIDE, SIDE + 1, dtype=jnp.int32)
    col_offsets = jax.random.randint(key_cols, (LR, LB, LINKS), -SIDE, SIDE + 1, dtype=jnp.int32)
    row_offsets = row_offsets.at[:, :, 0].set(SIDE)
    row_offsets = row_offsets.at[:, :, 1].set(-SIDE)
    col_offsets = col_offsets.at[:, :, 2].set(SIDE)
    col_offsets = col_offsets.at[:, :, 3].set(-SIDE)
    base_rows = jnp.arange(LR, dtype=jnp.int32)[:, None, None]
    base_cols = jnp.arange(LB, dtype=jnp.int32)[None, :, None]
    link_rows = (base_rows + row_offsets) % LR
    link_cols = (base_cols + col_offsets) % LB
    return jnp.stack([link_rows, link_cols], axis=-1).astype(jnp.int32)


def set_ends(array, stream_key, least, high):
    longest = array.shape.index(max(array.shape))
    spots = []
    for shift in (0, 1):
        where = [jax.random.randint(jax.random.fold_in(stream_key, axis), (), 0, length) for axis, length in enumerate(array.shape)]
        where[longest] = (where[longest] + shift) % array.shape[longest]
        spots.append(tuple(where))
    return array.at[spots[0]].set(least).at[spots[1]].set(high)


def block_levels(rng, dims, shards, low, high):
    level = 1.0
    for position, shards_of in shards:
        steps = jax.random.uniform(jax.random.fold_in(jax.random.fold_in(rng, 6), position), (shards_of,), jnp.float32, low / len(shards), high / len(shards))
        level = level * jnp.repeat(jnp.exp(steps), dims[position] // shards_of).reshape((-1,) + (1,) * (len(dims) - 1 - position))
    return level


def bell_draw(own_key, shape, scale, limit, cuts=(), kind=jnp.bfloat16):
    factor_of = block_levels(own_key, shape, cuts, -0.22, 0.18) if cuts else 1.0
    array = jax.random.normal(own_key, shape, jnp.float32) * scale * factor_of
    return jnp.minimum(jnp.maximum(array, -limit), limit).astype(kind)


def setup_inputs(seed: int = 0) -> dict:
    arg_keys = jax.random.split(jax.random.key(seed), 7)
    return {
        "right_side": bell_draw(arg_keys[0], (STEPS, CASES, LR, LB, BLOCK), 3.0, 16.0, ((0, 8), (2, 8), (3, 4)), jnp.float32),
        "stiffness": bell_draw(arg_keys[1], (LR, LB, LINKS, BLOCK, BLOCK), 0.007, 0.039794922, ((0, 8), (1, 4))),
        "segments": set_ends(jax.random.randint(arg_keys[2], (LR, LB, LINKS), 1, 5), jax.random.fold_in(arg_keys[2], 1), 1, 4).astype(jnp.int32),
        "connectivity": draw_connectivity(jax.random.fold_in(arg_keys[6], 71), 0),
        "lumped_mass": jnp.clip(jnp.exp(math.log(4.0) - 2.7725887 * jax.random.uniform(arg_keys[4], (LR, LB, BLOCK), jnp.float32) ** block_levels(arg_keys[4], (LR, LB, BLOCK), ((0, 8), (1, 4)), -0.2, 0.2)), 0.25, 4.0),
        "stiff_diag": jnp.clip(jnp.exp(math.log(16.0) - 2.3671236 * jax.random.uniform(arg_keys[5], (LR, LB, BLOCK), jnp.float32) ** block_levels(arg_keys[5], (LR, LB, BLOCK), ((0, 8), (1, 4)), -0.2, 0.2)), 1.5, 16.0),
    }


circulant_alpha = 0.5


def twiddle(left_ids, right_ids, length):
    product = (left_ids[:, None] * right_ids[None, :]) % length
    angles = (2.0 * math.pi / length) * product.astype(jnp.float32)
    return jnp.cos(angles), jnp.sin(angles)


def couple(values, stiffness, segments, connectivity):
    full_shape = values.shape
    columns = values.reshape((-1,) + full_shape[-3:])

    def one_row(lattice_row):
        link_rows = connectivity[lattice_row, :, :, 0]
        link_cols = connectivity[lattice_row, :, :, 1]
        picked = columns[:, link_rows, link_cols, :].astype(jnp.float32)
        matrices = stiffness[lattice_row].astype(jnp.float32)
        products = jnp.einsum("bnij,cbnj->cbni", matrices, picked, precision=lax.Precision.HIGHEST)
        factors = segments[lattice_row].astype(jnp.float32)[None, :, :, None]
        return jnp.sum(products * factors, axis=2)

    row_terms = lax.map(one_row, jnp.arange(full_shape[-3], dtype=jnp.int32))
    return jnp.transpose(row_terms, (1, 0, 2, 3)).reshape(full_shape)


def reference(right_side, stiffness, segments, connectivity, lumped_mass, stiff_diag):
    length = right_side.shape[0]
    highest = lax.Precision.HIGHEST
    decay_root = circulant_alpha ** (1.0 / length)
    log_rate = math.log(circulant_alpha) / length
    all_steps = jnp.arange(length, dtype=jnp.int32)
    weights = jnp.exp(all_steps.astype(jnp.float32) * log_rate)
    scaled = right_side * weights[:, None, None, None, None]
    flat_data = scaled.reshape(length, -1)
    cos_table, sin_table = twiddle(all_steps, all_steps, length)
    source_re = jnp.dot(cos_table, flat_data, precision=highest).reshape(right_side.shape)
    source_im = -jnp.dot(sin_table, flat_data, precision=highest).reshape(right_side.shape)
    angles = (2.0 * math.pi / length) * all_steps.astype(jnp.float32)
    shift_re = 1.0 - decay_root * jnp.cos(angles)
    shift_im = decay_root * jnp.sin(angles)
    diag_re = shift_re[:, None, None, None] * lumped_mass[None] + stiff_diag[None]
    diag_im = shift_im[:, None, None, None] * lumped_mass[None]
    modulus = diag_re * diag_re + diag_im * diag_im
    inverse_re = (diag_re / modulus)[:, None]
    inverse_im = (-diag_im / modulus)[:, None]
    solved_re = source_re * inverse_re - source_im * inverse_im
    solved_im = source_re * inverse_im + source_im * inverse_re
    for repeat in range(SWEEPS):
        rounded = jnp.stack([solved_re, solved_im]).astype(jnp.bfloat16)
        coupled = couple(rounded, stiffness, segments, connectivity)
        update_re = source_re - coupled[0]
        update_im = source_im - coupled[1]
        solved_re = update_re * inverse_re - update_im * inverse_im
        solved_im = update_re * inverse_im + update_im * inverse_re
    inv_cos, inv_sin = twiddle(all_steps, all_steps, length)
    signal = (jnp.dot(inv_cos, solved_re.reshape(length, -1), precision=highest)
              - jnp.dot(inv_sin, solved_im.reshape(length, -1), precision=highest)) / length
    signal = signal.reshape(right_side.shape)
    return signal * jnp.exp(-all_steps.astype(jnp.float32) * log_rate)[:, None, None, None, None]
```

```python
import math

import jax
import jax.numpy as jnp
import numpy as np
from jax import lax
from jax.experimental import pallas as pl
from jax.experimental.pallas import tpu as pltpu
from jax.sharding import PartitionSpec as P

MESH = pl.DeviceIdType.MESH
STEPS = 32
BLOCK = 384
LINKS = 10
CASES = 32
SITES = 4
TM = 8
ALPHA = 0.5
OWN_STEPS = STEPS // TM
OWN_CASES = CASES // TM
ROWS = OWN_STEPS * OWN_CASES
COLS = STEPS * OWN_CASES


def tables():
    rate = math.log(ALPHA) / STEPS
    root = ALPHA ** (1.0 / STEPS)
    n = np.arange(STEPS)
    k = np.arange(STEPS // 2)
    angle = 2.0 * np.pi / STEPS * ((n[:, None] * k[None, :]) % STEPS)
    real, imag = np.cos(angle), -np.sin(angle)
    alternate = np.where(n % 2 == 0, 1.0, -1.0)
    imag[:, 0] = alternate
    forward = np.concatenate([real, imag], axis=1) * np.exp(n * rate)[:, None]
    back_real, back_imag = 2.0 * np.cos(angle), -2.0 * np.sin(angle)
    back_real[:, 0] = 1.0
    back_imag[:, 0] = alternate
    backward = np.concatenate([back_real, back_imag], axis=1) / STEPS * np.exp(-n * rate)[:, None]
    eye = np.eye(OWN_CASES)
    theta = 2.0 * np.pi * k / STEPS
    shift_re = np.concatenate([1.0 - root * np.cos(theta)] * 2)
    shift_re[STEPS // 2] = 1.0 + root
    shift_im = np.concatenate([root * np.sin(theta), -root * np.sin(theta)])
    shift_im[0] = shift_im[STEPS // 2] = 0.0
    shifts = np.zeros((8, COLS))
    shifts[0] = np.repeat(shift_re, OWN_CASES)
    shifts[1] = np.repeat(shift_im, OWN_CASES)
    as_f32 = lambda a: np.asarray(a, np.float32)
    return as_f32(np.kron(forward, eye)), as_f32(np.kron(backward, eye)), as_f32(shifts)


def kernel(xs, stiff_hbm, seg, conn, mass, diag, fwd, bwd, shifts, out,
           stiff, recv, ext_first, ext_second, source, coef_a, coef_b, result,
           stiff_sem, in_send, in_recv, own_sem, halo_send, halo_recv, out_send, out_recv):
    tm, row, blk = lax.axis_index("tm"), lax.axis_index("row"), lax.axis_index("blk")
    odd = lax.rem(row, 2)
    partner = {"row": row + 1 - 2 * odd}
    outer = {"row": lax.rem(row + 7 + 2 * odd, 8)}
    ahead = {"blk": lax.rem(blk + 1, 4)}
    behind = {"blk": lax.rem(blk + 3, 4)}

    stiff_copy = pltpu.make_async_copy(stiff_hbm, stiff, stiff_sem)
    stiff_copy.start()

    barrier = pltpu.get_barrier_semaphore()
    for step in range(1, TM):
        pl.semaphore_signal(barrier, inc=1, device_id={"tm": lax.rem(tm + step, TM)}, device_id_type=MESH)
    for near in (partner, outer, ahead, behind):
        pl.semaphore_signal(barrier, inc=1, device_id=near, device_id_type=MESH)
    pl.semaphore_wait(barrier, TM - 1 + 4)

    def in_copy(site, step):
        to = lax.rem(tm + step, TM)
        return pltpu.make_async_remote_copy(
            src_ref=xs.at[to, site], dst_ref=recv.at[site, pl.ds(pl.multiple_of(tm * ROWS, ROWS), ROWS)],
            send_sem=in_send.at[site, step], recv_sem=in_recv.at[site, step],
            device_id={"tm": to}, device_id_type=MESH)

    def in_own(site):
        return pltpu.make_async_copy(
            xs.at[tm, site], recv.at[site, pl.ds(pl.multiple_of(tm * ROWS, ROWS), ROWS)], own_sem.at[site])

    def start_in(site, carry):
        in_own(site).start()
        for step in range(1, TM):
            in_copy(site, step).start()
        return carry

    lax.fori_loop(0, SITES, start_in, 0)

    for site in range(SITES):
        a, b = divmod(site, 2)
        mass_t = jnp.broadcast_to(mass[a, b:b + 1, :], (COLS, BLOCK)).T
        diag_t = jnp.broadcast_to(diag[a, b:b + 1, :], (COLS, BLOCK)).T
        diag_re = shifts[0:1, :] * mass_t + diag_t
        diag_im = shifts[1:2, :] * mass_t
        modulus = diag_re * diag_re + diag_im * diag_im
        coef_a[site] = diag_re / modulus
        coef_b[site] = diag_im / modulus

    def apply_inverse(site, update):
        return coef_a[site] * update + coef_b[site] * pltpu.roll(update, COLS // 2, 1)

    exts = (ext_first, ext_second)

    def halo_copy(sweep, kind, site):
        source_at, target_at, to = (
            ((0, 0), (1, 0), partner),
            ((0, 0), (2, 0), outer),
            ((0, 0), (0, 1), ahead),
            ((0, 0), (0, 2), behind),
            ((2, 0), (2, 1), ahead),
            ((2, 0), (2, 2), behind),
            ((0, 1), (1, 1), partner),
            ((0, 2), (1, 2), partner),
        )[kind]
        at = lambda place: exts[sweep].at[place[0] * 3 + place[1], site]
        return pltpu.make_async_remote_copy(
            src_ref=at(source_at), dst_ref=at(target_at),
            send_sem=halo_send.at[sweep, kind, site], recv_sem=halo_recv.at[sweep, kind, site],
            device_id=to, device_id_type=MESH)

    def send_own(sweep, site):
        for kind in (1, 2, 3, 0):
            halo_copy(sweep, kind, site).start()

    def pass_on(sweep):
        def forward(site, carry):
            halo_copy(sweep, 1, site).wait_recv()
            halo_copy(sweep, 4, site).start()
            halo_copy(sweep, 5, site).start()
            halo_copy(sweep, 2, site).wait_recv()
            halo_copy(sweep, 6, site).start()
            halo_copy(sweep, 3, site).wait_recv()
            halo_copy(sweep, 7, site).start()
            return carry

        def finish(site, carry):
            for kind in (0, 4, 5, 6, 7):
                halo_copy(sweep, kind, site).wait_recv()
            return carry

        lax.fori_loop(0, SITES, forward, 0)
        lax.fori_loop(0, SITES, finish, 0)

    def transform(site, carry):
        in_own(site).wait()
        for step in range(1, TM):
            in_copy(site, step).wait_recv()
        spectrum = jnp.dot(recv[site].T, fwd[...], precision=lax.Precision.HIGHEST, preferred_element_type=jnp.float32)
        source[site] = spectrum
        ext_first[0, site] = apply_inverse(site, spectrum).astype(jnp.bfloat16)
        send_own(0, site)
        return carry

    lax.fori_loop(0, SITES, transform, 0)
    pass_on(0)
    stiff_copy.wait()

    def relaxed(sweep, site):
        total = jnp.zeros((BLOCK, COLS), jnp.float32)
        for link in range(LINKS):
            place = site * LINKS + link
            up = lax.rem(conn[place * 2] - 2 * row + 18, 16)
            across = lax.rem(conn[place * 2 + 1] - 2 * blk + 10, 8)
            up_block, across_block = up // 2, across // 2
            row_place = jnp.where(up_block == 1, 0, jnp.where(up_block == 2 - 2 * odd, 1, 2))
            col_place = jnp.where(across_block == 1, 0, jnp.where(across_block == 0, 1, 2))
            named = exts[sweep][row_place * 3 + col_place, lax.rem(up, 2) * 2 + lax.rem(across, 2)]
            product = jnp.dot(stiff[place], named, preferred_element_type=jnp.float32)
            total = total + product * seg[place].astype(jnp.float32)
        return apply_inverse(site, source[site] - total)

    def first_sweep(site, carry):
        ext_second[0, site] = relaxed(0, site).astype(jnp.bfloat16)
        send_own(1, site)
        return carry

    lax.fori_loop(0, SITES, first_sweep, 0)
    pass_on(1)

    def out_copy(site, step):
        to = lax.rem(tm + step, TM)
        return pltpu.make_async_remote_copy(
            src_ref=result.at[site, pl.ds(pl.multiple_of(to * ROWS, ROWS), ROWS)], dst_ref=out.at[tm, site],
            send_sem=out_send.at[site, step], recv_sem=out_recv.at[site, step],
            device_id={"tm": to}, device_id_type=MESH)

    def out_own(site):
        return pltpu.make_async_copy(
            result.at[site, pl.ds(pl.multiple_of(tm * ROWS, ROWS), ROWS)], out.at[tm, site], own_sem.at[site])

    def second_sweep(site, carry):
        signal = lax.dot_general(bwd[...], relaxed(1, site), (((1,), (1,)), ((), ())),
                                 precision=lax.Precision.HIGHEST, preferred_element_type=jnp.float32)
        result[site] = signal
        out_own(site).start()
        for step in range(1, TM):
            out_copy(site, step).start()
        return carry

    lax.fori_loop(0, SITES, second_sweep, 0)

    def drain(site, carry):
        for sweep in range(2):
            for kind in range(8):
                halo_copy(sweep, kind, site).wait_send()
        for step in range(1, TM):
            in_copy(site, step).wait_send()
            out_copy(site, step).wait_send()
            out_copy(site, step).wait_recv()
        out_own(site).wait()
        return carry

    lax.fori_loop(0, SITES, drain, 0)


def shards(right_side, stiffness, segments, connectivity, lumped_mass, stiff_diag):
    fwd, bwd, shifts = tables()
    blocks = right_side.reshape(OWN_STEPS, TM, OWN_CASES, SITES, BLOCK)
    xs = jnp.transpose(blocks, (1, 3, 0, 2, 4)).reshape(TM, SITES, ROWS, BLOCK)
    vmem = pl.BlockSpec(memory_space=pltpu.VMEM)
    smem = pl.BlockSpec(memory_space=pltpu.SMEM)
    anywhere = pl.BlockSpec(memory_space=pl.ANY)
    dma = pltpu.SemaphoreType.DMA
    out = pl.pallas_call(
        kernel,
        out_shape=jax.ShapeDtypeStruct((TM, SITES, ROWS, BLOCK), jnp.float32),
        in_specs=[anywhere, anywhere, smem, smem, vmem, vmem, vmem, vmem, vmem],
        out_specs=vmem,
        scratch_shapes=[
            pltpu.VMEM((SITES * LINKS, BLOCK, BLOCK), jnp.bfloat16),
            pltpu.VMEM((SITES, COLS, BLOCK), jnp.float32),
            pltpu.VMEM((9, SITES, BLOCK, COLS), jnp.bfloat16),
            pltpu.VMEM((9, SITES, BLOCK, COLS), jnp.bfloat16),
            pltpu.VMEM((SITES, BLOCK, COLS), jnp.float32),
            pltpu.VMEM((SITES, BLOCK, COLS), jnp.float32),
            pltpu.VMEM((SITES, BLOCK, COLS), jnp.float32),
            pltpu.VMEM((SITES, COLS, BLOCK), jnp.float32),
            dma,
            dma((SITES, TM)),
            dma((SITES, TM)),
            dma((SITES,)),
            dma((2, 8, SITES)),
            dma((2, 8, SITES)),
            dma((SITES, TM)),
            dma((SITES, TM)),
        ],
        compiler_params=pltpu.CompilerParams(
            collective_id=0, has_side_effects=True, vmem_limit_bytes=48 * 2**20),
    )(xs, stiffness.reshape(SITES * LINKS, BLOCK, BLOCK), segments.reshape(-1), connectivity.reshape(-1),
      lumped_mass, stiff_diag, fwd, bwd, shifts)
    steps = out.reshape(TM, SITES, OWN_STEPS, OWN_CASES, BLOCK)
    return jnp.transpose(steps, (2, 0, 3, 1, 4)).reshape(right_side.shape)


def solution(mesh):
    placed = (
        P("tm", None, "row", "blk", None),
        P("row", "blk", None, None, None),
        P("row", "blk", None),
        P("row", "blk", None, None),
        P("row", "blk", None),
        P("row", "blk", None),
    )
    return jax.shard_map(
        shards,
        mesh=mesh,
        in_specs=placed,
        out_specs=P("tm", None, "row", "blk", None),
        check_vma=False,
    )
```

```python
import math

import jax
import jax.numpy as jnp
import numpy as np
from jax import lax
from jax.experimental import pallas as pl
from jax.experimental.pallas import tpu as pltpu
from jax.sharding import PartitionSpec as P

MESH = pl.DeviceIdType.MESH
STEPS = 32
BLOCK = 384
LINKS = 10
CASES = 32
SIDE = 2
CHUNKS = 2
GROUPS = CHUNKS * SIDE
TM = 8
ALPHA = 0.5
OWN_STEPS = STEPS // TM
OWN_CASES = CASES // TM
PAIR = OWN_CASES // CHUNKS
ROWS = OWN_STEPS * PAIR * SIDE
COLS = STEPS * PAIR * SIDE


def tables():
    rate = math.log(ALPHA) / STEPS
    root = ALPHA ** (1.0 / STEPS)
    n = np.arange(STEPS)
    k = np.arange(STEPS // 2)
    angle = 2.0 * np.pi / STEPS * ((n[:, None] * k[None, :]) % STEPS)
    real, imag = np.cos(angle), -np.sin(angle)
    alternate = np.where(n % 2 == 0, 1.0, -1.0)
    imag[:, 0] = alternate
    forward = np.concatenate([real, imag], axis=1) * np.exp(n * rate)[:, None]
    back_real, back_imag = 2.0 * np.cos(angle), -2.0 * np.sin(angle)
    back_real[:, 0] = 1.0
    back_imag[:, 0] = alternate
    backward = np.concatenate([back_real, back_imag], axis=1) / STEPS * np.exp(-n * rate)[:, None]
    eye = np.eye(PAIR * SIDE)
    theta = 2.0 * np.pi * k / STEPS
    shift_re = np.concatenate([1.0 - root * np.cos(theta)] * 2)
    shift_re[STEPS // 2] = 1.0 + root
    shift_im = np.concatenate([root * np.sin(theta), -root * np.sin(theta)])
    shift_im[0] = shift_im[STEPS // 2] = 0.0
    shifts = np.zeros((8, COLS))
    shifts[0] = np.repeat(shift_re, PAIR * SIDE)
    shifts[1] = np.repeat(shift_im, PAIR * SIDE)
    as_f32 = lambda a: np.asarray(a, np.float32)
    return as_f32(np.kron(forward, eye)), as_f32(np.kron(backward, eye)), as_f32(shifts)


def kernel(right, stiff_hbm, seg, conn, mass_hbm, diag_hbm, fwd_hbm, bwd_hbm, shifts_hbm, out,
           stiff, mass, diag, fwd, bwd, shifts, given, coded, recv, scale_given, scale_recv,
           ext00, ext01, ext10, ext11, source, coef_a, coef_b,
           result, landed, scale_result, scale_landed, final,
           load_sem, in_send, in_recv, own_sem, scale_send, scale_sem, halo_send, halo_recv,
           out_send, out_recv, out_scale_send, out_scale_recv):
    tm, row, blk = lax.axis_index("tm"), lax.axis_index("row"), lax.axis_index("blk")
    odd = lax.rem(row, 2)
    partner = {"row": row + 1 - 2 * odd}
    outer = {"row": lax.rem(row + 7 + 2 * odd, 8)}
    ahead = {"blk": lax.rem(blk + 1, 4)}
    behind = {"blk": lax.rem(blk + 3, 4)}
    exts = ((ext00, ext01), (ext10, ext11))

    loads = [
        pltpu.make_async_copy(source_ref, target_ref, load_sem.at[place])
        for place, (source_ref, target_ref) in enumerate((
            (right, given), (mass_hbm, mass), (diag_hbm, diag), (shifts_hbm, shifts), (fwd_hbm, fwd), (bwd_hbm, bwd), (stiff_hbm, stiff)))
    ]
    for load in loads:
        load.start()

    barrier = pltpu.get_barrier_semaphore()
    for step in range(1, TM):
        pl.semaphore_signal(barrier, inc=1, device_id={"tm": lax.rem(tm + step, TM)}, device_id_type=MESH)
    for near in (partner, outer, ahead, behind):
        pl.semaphore_signal(barrier, inc=1, device_id=near, device_id_type=MESH)

    lane = lax.broadcasted_iota(jnp.int32, (1, COLS), 1)

    def encode(value):
        largest = jnp.maximum(jnp.max(jnp.abs(value), axis=1, keepdims=True), 1e-30)
        whole = jnp.round(value * (32767.0 / largest)).astype(jnp.int32).astype(jnp.int16)
        scales = jnp.broadcast_to(largest * (1.0 / 32767.0), (COLS, COLS)).T
        return whole, scales[0:1, :]

    def own_scales(row_from):
        scales = jnp.zeros((1, COLS), jnp.float32)
        for step in range(TM):
            moved = pltpu.roll(row_from(step), lax.rem((step - tm + TM) * ROWS, COLS), 1)
            scales = jnp.where(lane // ROWS == step, moved, scales)
        return scales

    loads[0].wait()

    def code(group, carry):
        chunk, a = group // SIDE, lax.rem(group, SIDE)
        value = jnp.concatenate([given[:, to, chunk, :, a].reshape(ROWS, BLOCK) for to in range(TM)], axis=0)
        coded[group], scale_given[group] = encode(value)
        return carry

    lax.fori_loop(0, GROUPS, code, 0)
    scale_recv[tm] = scale_given[...]
    pl.semaphore_wait(barrier, TM - 1 + 4)

    def scale_copy(step):
        return pltpu.make_async_remote_copy(
            src_ref=scale_given, dst_ref=scale_recv.at[tm], send_sem=scale_send.at[step], recv_sem=scale_sem.at[step],
            device_id={"tm": lax.rem(tm + step, TM)}, device_id_type=MESH)

    def rows_of(owner):
        return pl.ds(pl.multiple_of(owner * ROWS, ROWS), ROWS)

    def in_copy(group, step):
        to = lax.rem(tm + step, TM)
        return pltpu.make_async_remote_copy(
            src_ref=coded.at[group, rows_of(to)], dst_ref=recv.at[group, rows_of(tm)],
            send_sem=in_send.at[group, step], recv_sem=in_recv.at[group, step],
            device_id={"tm": to}, device_id_type=MESH)

    def in_own(group):
        return pltpu.make_async_copy(coded.at[group, rows_of(tm)], recv.at[group, rows_of(tm)], own_sem.at[group])

    def start_in(group, carry):
        in_own(group).start()
        for step in range(1, TM):
            in_copy(group, step).start()
        return carry

    for step in range(1, TM):
        scale_copy(step).start()
    lax.fori_loop(0, GROUPS, start_in, 0)

    first_block = lax.rem(lane, 2) == 0
    for load in loads[1:4]:
        load.wait()

    def by_column(ref, lattice_row):
        column = lambda b: jnp.broadcast_to(ref[lattice_row, b:b + 1, :], (COLS, BLOCK)).T
        return jnp.where(first_block, column(0), column(1))

    for a in range(SIDE):
        mass_t, diag_t = by_column(mass, a), by_column(diag, a)
        diag_re = shifts[0:1, :] * mass_t + diag_t
        diag_im = shifts[1:2, :] * mass_t
        modulus = diag_re * diag_re + diag_im * diag_im
        coef_a[a] = diag_re / modulus
        coef_b[a] = diag_im / modulus
    for load in loads[4:6]:
        load.wait()

    def apply_inverse(a, update):
        return coef_a[a] * update + coef_b[a] * pltpu.roll(update, COLS // 2, 1)

    def halo_copy(sweep, kind, chunk, a):
        source_at, target_at, to = (
            ((0, 0), (1, 0), partner),
            ((0, 0), (2, 0), outer),
            ((0, 0), (0, 1), ahead),
            ((0, 0), (0, 2), behind),
            ((2, 0), (2, 1), ahead),
            ((2, 0), (2, 2), behind),
            ((0, 1), (1, 1), partner),
            ((0, 2), (1, 2), partner),
        )[kind]
        at = lambda place: exts[sweep][chunk].at[place[0] * 3 + place[1], a]
        group = chunk * SIDE + a
        return pltpu.make_async_remote_copy(
            src_ref=at(source_at), dst_ref=at(target_at),
            send_sem=halo_send.at[sweep, kind, group], recv_sem=halo_recv.at[sweep, kind, group],
            device_id=to, device_id_type=MESH)

    def send_own(sweep, chunk, a):
        for kind in (1, 2, 3, 0):
            halo_copy(sweep, kind, chunk, a).start()

    def over_rows(body):
        def step(a, carry):
            body(a)
            return carry
        lax.fori_loop(0, SIDE, step, 0)

    def pass_across(sweep, chunk):
        def body(a):
            halo_copy(sweep, 1, chunk, a).wait_recv()
            halo_copy(sweep, 4, chunk, a).start()
            halo_copy(sweep, 5, chunk, a).start()
        over_rows(body)

    def pass_partner(sweep, chunk):
        def body(a):
            halo_copy(sweep, 2, chunk, a).wait_recv()
            halo_copy(sweep, 6, chunk, a).start()
            halo_copy(sweep, 3, chunk, a).wait_recv()
            halo_copy(sweep, 7, chunk, a).start()
        over_rows(body)

    def arrive(sweep, chunk):
        def body(a):
            for kind in (0, 4, 5, 6, 7):
                halo_copy(sweep, kind, chunk, a).wait_recv()
        over_rows(body)

    def transform(chunk):
        def body(a):
            group = chunk * SIDE + a
            in_own(group).wait()
            for step in range(1, TM):
                in_copy(group, step).wait_recv()
            steps = recv[group].astype(jnp.int32).astype(jnp.float32).T * own_scales(lambda step: scale_recv[step, group])
            spectrum = jnp.dot(steps, fwd[...],
                               precision=lax.Precision.HIGHEST, preferred_element_type=jnp.float32)
            source[group] = spectrum
            exts[0][chunk][0, a] = apply_inverse(a, spectrum).astype(jnp.bfloat16)
            send_own(0, chunk, a)
        over_rows(body)

    def relaxed(sweep, chunk, a):
        parts = []
        for b in range(SIDE):
            total = jnp.zeros((BLOCK, COLS), jnp.float32)
            for link in range(LINKS):
                up = lax.rem(conn[a, b, 0, link] - 2 * row + 18, 16)
                across = lax.rem(conn[a, b, 1, link] - 2 * blk + 10, 8)
                up_block, across_block = up // 2, across // 2
                row_place = jnp.where(up_block == 1, 0, jnp.where(up_block == 2 - 2 * odd, 1, 2))
                col_place = jnp.where(across_block == 1, 0, jnp.where(across_block == 0, 1, 2))
                named = exts[sweep][chunk][row_place * 3 + col_place, lax.rem(up, 2)]
                product = jnp.dot(stiff[(a * SIDE + b) * LINKS + link], named, preferred_element_type=jnp.float32)
                factor = seg[a, b, link].astype(jnp.float32)
                total = total + product * jnp.where(first_block == (lax.rem(across, 2) == 0), factor, 0.0)
            parts.append(total)
        mine = jnp.where(first_block, parts[0], parts[1])
        other = jnp.where(first_block, parts[1], parts[0])
        other = jnp.where(first_block, pltpu.roll(other, COLS - 1, 1), pltpu.roll(other, 1, 1))
        return apply_inverse(a, source[chunk * SIDE + a] - (mine + other))

    def first_sweep(chunk):
        def body(a):
            exts[1][chunk][0, a] = relaxed(0, chunk, a).astype(jnp.bfloat16)
            send_own(1, chunk, a)
        over_rows(body)

    def out_copy(group, step):
        to = lax.rem(tm + step, TM)
        return pltpu.make_async_remote_copy(
            src_ref=result.at[group, rows_of(to)], dst_ref=landed.at[group, rows_of(tm)],
            send_sem=out_send.at[group, step], recv_sem=out_recv.at[group, step],
            device_id={"tm": to}, device_id_type=MESH)

    def out_scale(group, step):
        return pltpu.make_async_remote_copy(
            src_ref=scale_result.at[group], dst_ref=scale_landed.at[group, tm],
            send_sem=out_scale_send.at[group, step], recv_sem=out_scale_recv.at[group, step],
            device_id={"tm": lax.rem(tm + step, TM)}, device_id_type=MESH)

    def out_own(group):
        return pltpu.make_async_copy(result.at[group, rows_of(tm)], landed.at[group, rows_of(tm)], own_sem.at[group])

    def second_sweep(chunk):
        def body(a):
            group = chunk * SIDE + a
            signal = lax.dot_general(bwd[...], relaxed(1, chunk, a), (((1,), (1,)), ((), ())),
                                     precision=lax.Precision.HIGHEST, preferred_element_type=jnp.float32)
            result[group], scale_result[group] = encode(signal)
            scale_landed[group, tm] = scale_result[group]
            for step in range(1, TM):
                out_scale(group, step).start()
                out_copy(group, step).start()
            out_own(group).start()
        over_rows(body)

    def final_copy(chunk, a):
        return pltpu.make_async_copy(
            final.at[:, :, chunk, :, a], out.at[:, :, chunk, :, a], in_send.at[chunk * SIDE + a, 0])

    def finish(chunk):
        def body(a):
            group = chunk * SIDE + a
            out_own(group).wait()
            for step in range(1, TM):
                out_copy(group, step).wait_recv()
                out_scale(group, step).wait_recv()
            scales = jnp.broadcast_to(own_scales(lambda step: scale_landed[group, step]), (COLS, COLS)).T
            value = landed[group].astype(jnp.int32).astype(jnp.float32) * jnp.concatenate([scales] * (BLOCK // COLS), axis=1)
            for step in range(TM):
                part = value[step * ROWS:(step + 1) * ROWS]
                final[:, step, chunk, :, a] = part.reshape(OWN_STEPS, PAIR, SIDE, BLOCK)
            final_copy(chunk, a).start()
        over_rows(body)

    for step in range(1, TM):
        scale_copy(step).wait_recv()
    transform(0)
    pass_across(0, 0)
    transform(1)
    pass_partner(0, 0)
    pass_across(0, 1)
    arrive(0, 0)
    loads[6].wait()
    first_sweep(0)
    pass_partner(0, 1)
    pass_across(1, 0)
    arrive(0, 1)
    first_sweep(1)
    pass_partner(1, 0)
    pass_across(1, 1)
    arrive(1, 0)
    second_sweep(0)
    pass_partner(1, 1)
    arrive(1, 1)
    second_sweep(1)

    finish(0)
    finish(1)

    def drain(group, carry):
        for step in range(1, TM):
            in_copy(group, step).wait_send()
            out_copy(group, step).wait_send()
            out_scale(group, step).wait_send()
        final_copy(group // SIDE, lax.rem(group, SIDE)).wait()
        return carry

    for step in range(1, TM):
        scale_copy(step).wait_send()
    lax.fori_loop(0, GROUPS, drain, 0)
    for sweep in range(2):
        for chunk in range(CHUNKS):
            over_rows(lambda a: [halo_copy(sweep, kind, chunk, a).wait_send() for kind in range(8)])


def shards(right_side, stiffness, segments, connectivity, lumped_mass, stiff_diag):
    smem = pl.BlockSpec(memory_space=pltpu.SMEM)
    hbm = pl.BlockSpec(memory_space=pltpu.HBM)
    dma = pltpu.SemaphoreType.DMA
    ext = pltpu.VMEM((9, SIDE, BLOCK, COLS), jnp.bfloat16)
    split = (OWN_STEPS, TM, CHUNKS, PAIR, SIDE, SIDE, BLOCK)
    rows = pltpu.VMEM((GROUPS, COLS, BLOCK), jnp.int16)
    result = pl.pallas_call(
        kernel,
        out_shape=jax.ShapeDtypeStruct(split, jnp.float32),
        in_specs=[hbm, hbm, smem, smem, hbm, hbm, hbm, hbm, hbm],
        out_specs=hbm,
        scratch_shapes=[
            pltpu.VMEM((SIDE * SIDE * LINKS, BLOCK, BLOCK), jnp.bfloat16),
            pltpu.VMEM(lumped_mass.shape, jnp.float32),
            pltpu.VMEM(stiff_diag.shape, jnp.float32),
            pltpu.VMEM((COLS, COLS), jnp.float32),
            pltpu.VMEM((COLS, COLS), jnp.float32),
            pltpu.VMEM((8, COLS), jnp.float32),
            pltpu.VMEM(split, jnp.float32),
            rows,
            rows,
            pltpu.VMEM((GROUPS, 1, COLS), jnp.float32),
            pltpu.VMEM((TM, GROUPS, 1, COLS), jnp.float32),
            ext, ext, ext, ext,
            pltpu.VMEM((GROUPS, BLOCK, COLS), jnp.float32),
            pltpu.VMEM((SIDE, BLOCK, COLS), jnp.float32),
            pltpu.VMEM((SIDE, BLOCK, COLS), jnp.float32),
            rows,
            rows,
            pltpu.VMEM((GROUPS, 1, COLS), jnp.float32),
            pltpu.VMEM((GROUPS, TM, 1, COLS), jnp.float32),
            pltpu.VMEM(split, jnp.float32),
            dma((7,)),
            dma((GROUPS, TM)),
            dma((GROUPS, TM)),
            dma((GROUPS,)),
            dma((TM,)),
            dma((TM,)),
            dma((2, 8, GROUPS)),
            dma((2, 8, GROUPS)),
            dma((GROUPS, TM)),
            dma((GROUPS, TM)),
            dma((GROUPS, TM)),
            dma((GROUPS, TM)),
        ],
        compiler_params=pltpu.CompilerParams(
            collective_id=0, has_side_effects=True, vmem_limit_bytes=60 * 2**20),
    )(right_side.reshape(split), stiffness.reshape(SIDE * SIDE * LINKS, BLOCK, BLOCK), segments,
      jnp.transpose(connectivity, (0, 1, 3, 2)), lumped_mass, stiff_diag, *tables())
    return result.reshape(right_side.shape)


def solution(mesh):
    placed = (
        P("tm", None, "row", "blk", None),
        P("row", "blk", None, None, None),
        P("row", "blk", None),
        P("row", "blk", None, None),
        P("row", "blk", None),
        P("row", "blk", None),
    )
    return jax.shard_map(
        shards,
        mesh=mesh,
        in_specs=placed,
        out_specs=P("tm", None, "row", "blk", None),
        check_vma=False,
    )
```

```python
import math

import jax
import jax.numpy as jnp
import numpy as np
from jax import lax
from jax.experimental import pallas as pl
from jax.experimental.pallas import tpu as pltpu
from jax.sharding import PartitionSpec as P

MESH = pl.DeviceIdType.MESH
STEPS = 32
BLOCK = 384
LINKS = 10
CASES = 32
SIDE = 2
CHUNKS = 2
GROUPS = CHUNKS * SIDE
TM = 8
ALPHA = 0.5
OWN_STEPS = STEPS // TM
OWN_CASES = CASES // TM
PAIR = OWN_CASES // CHUNKS
ROWS = OWN_STEPS * PAIR * SIDE
COLS = STEPS * PAIR * SIDE


def tables():
    rate = math.log(ALPHA) / STEPS
    root = ALPHA ** (1.0 / STEPS)
    n = np.arange(STEPS)
    k = np.arange(STEPS // 2)
    angle = 2.0 * np.pi / STEPS * ((n[:, None] * k[None, :]) % STEPS)
    real, imag = np.cos(angle), -np.sin(angle)
    alternate = np.where(n % 2 == 0, 1.0, -1.0)
    imag[:, 0] = alternate
    forward = np.concatenate([real, imag], axis=1) * np.exp(n * rate)[:, None]
    back_real, back_imag = 2.0 * np.cos(angle), -2.0 * np.sin(angle)
    back_real[:, 0] = 1.0
    back_imag[:, 0] = alternate
    backward = np.concatenate([back_real, back_imag], axis=1) / STEPS * np.exp(-n * rate)[:, None]
    eye = np.eye(PAIR * SIDE)
    theta = 2.0 * np.pi * k / STEPS
    shift_re = np.concatenate([1.0 - root * np.cos(theta)] * 2)
    shift_re[STEPS // 2] = 1.0 + root
    shift_im = np.concatenate([root * np.sin(theta), -root * np.sin(theta)])
    shift_im[0] = shift_im[STEPS // 2] = 0.0
    shifts = np.zeros((8, COLS))
    shifts[0] = np.repeat(shift_re, PAIR * SIDE)
    shifts[1] = np.repeat(shift_im, PAIR * SIDE)
    as_f32 = lambda a: np.asarray(a, np.float32)
    return as_f32(np.kron(forward, eye)), as_f32(np.kron(backward, eye)), as_f32(shifts)


def own_scales(tm, row_from):
    lane = lax.broadcasted_iota(jnp.int32, (1, COLS), 1)
    scales = jnp.zeros((1, COLS), jnp.float32)
    for step in range(TM):
        moved = pltpu.roll(row_from(step), lax.rem((step - tm + TM) * ROWS, COLS), 1)
        scales = jnp.where(lane // ROWS == step, moved, scales)
    return scales


OTHERS = range(1, TM)


def other(tm, step):
    half, place = tm // 4, lax.rem(tm, 4)
    return lax.rem(half + (step <= 4), 2) * 4 + lax.rem(place + (step if step <= 4 else step - 4), 4)


def copy_kernel(given, out, held, load_sem, store_sem):
    load = [pltpu.make_async_copy(given.at[step], held.at[step], load_sem.at[step]) for step in range(OWN_STEPS)]
    store = [pltpu.make_async_copy(held.at[step], out.at[step], store_sem.at[step]) for step in range(OWN_STEPS)]
    for copy in load:
        copy.start()
    for here, there in zip(load, store):
        here.wait()
        there.start()
    for copy in store:
        copy.wait()


def kernel(right, stiff_hbm, seg_hbm, conn_hbm, mass_hbm, diag_hbm, fwd_hbm, bwd_hbm, shifts_hbm, out,
           stiff, seg, conn, mass, diag, fwd, bwd, shifts, given, coded, recv, scale_given, scale_recv,
           ext00, ext01, ext10, ext11, source, coef_a, coef_b,
           result, scale_result, landed, scale_landed, final,
           load_sem, in_send, in_recv, own_sem, own_scale_sem, scale_send, scale_sem, halo_send, halo_recv,
           out_send, out_recv, out_scale_send, out_scale_recv, final_sem):
    tm, row, blk = lax.axis_index("tm"), lax.axis_index("row"), lax.axis_index("blk")
    odd = lax.rem(row, 2)
    partner = {"row": row + 1 - 2 * odd}
    outer = {"row": lax.rem(row + 7 + 2 * odd, 8)}
    ahead = {"blk": lax.rem(blk + 1, 4)}
    behind = {"blk": lax.rem(blk + 3, 4)}
    exts = ((ext00, ext01), (ext10, ext11))

    barrier = pltpu.get_barrier_semaphore()
    for step in OTHERS:
        pl.semaphore_signal(barrier, inc=1, device_id={"tm": other(tm, step)}, device_id_type=MESH)
    for near in (partner, outer, ahead, behind):
        pl.semaphore_signal(barrier, inc=1, device_id=near, device_id_type=MESH)

    loads = [
        pltpu.make_async_copy(source_ref, target_ref, load_sem.at[place])
        for place, (source_ref, target_ref) in enumerate((
            (right, given), (mass_hbm, mass), (diag_hbm, diag), (shifts_hbm, shifts), (fwd_hbm, fwd), (bwd_hbm, bwd),
            (seg_hbm, seg), (conn_hbm, conn), (stiff_hbm, stiff)))
    ]
    for load in loads:
        load.start()

    lane = lax.broadcasted_iota(jnp.int32, (1, COLS), 1)

    def encode(value):
        largest = jnp.maximum(jnp.max(jnp.abs(value), axis=1, keepdims=True), 1e-30)
        whole = jnp.round(value * (32767.0 / largest)).astype(jnp.int32).astype(jnp.int16)
        scales = jnp.broadcast_to(largest * (1.0 / 32767.0), (COLS, COLS)).T
        return whole, scales[0:1, :]

    loads[0].wait()

    def code(group, carry):
        chunk, a = group // SIDE, lax.rem(group, SIDE)
        value = jnp.concatenate([given[:, to, chunk, :, a].reshape(ROWS, BLOCK) for to in range(TM)], axis=0)
        coded[group], scale_given[group] = encode(value)
        return carry

    lax.fori_loop(0, GROUPS, code, 0)
    scale_recv[tm] = scale_given[...]
    pl.semaphore_wait(barrier, TM - 1 + 4)

    def scale_copy(step):
        return pltpu.make_async_remote_copy(
            src_ref=scale_given, dst_ref=scale_recv.at[tm], send_sem=scale_send.at[step], recv_sem=scale_sem.at[step],
            device_id={"tm": other(tm, step)}, device_id_type=MESH)

    def rows_of(owner):
        return pl.ds(pl.multiple_of(owner * ROWS, ROWS), ROWS)

    def in_copy(group, step):
        to = other(tm, step)
        return pltpu.make_async_remote_copy(
            src_ref=coded.at[group, rows_of(to)], dst_ref=recv.at[group, rows_of(tm)],
            send_sem=in_send.at[group, step], recv_sem=in_recv.at[group, step],
            device_id={"tm": to}, device_id_type=MESH)

    def in_own(group):
        return pltpu.make_async_copy(coded.at[group, rows_of(tm)], recv.at[group, rows_of(tm)], own_sem.at[group])

    def start_in(group, carry):
        in_own(group).start()
        for step in OTHERS:
            in_copy(group, step).start()
        return carry

    for step in OTHERS:
        scale_copy(step).start()
    lax.fori_loop(0, GROUPS, start_in, 0)

    first_block = lax.rem(lane, 2) == 0
    for load in loads[1:4]:
        load.wait()

    def by_column(ref, lattice_row):
        column = lambda b: jnp.broadcast_to(ref[lattice_row, b:b + 1, :], (COLS, BLOCK)).T
        return jnp.where(first_block, column(0), column(1))

    for a in range(SIDE):
        mass_t, diag_t = by_column(mass, a), by_column(diag, a)
        diag_re = shifts[0:1, :] * mass_t + diag_t
        diag_im = shifts[1:2, :] * mass_t
        modulus = diag_re * diag_re + diag_im * diag_im
        coef_a[a] = diag_re / modulus
        coef_b[a] = diag_im / modulus
    for load in loads[4:6]:
        load.wait()

    def apply_inverse(a, update):
        return coef_a[a] * update + coef_b[a] * pltpu.roll(update, COLS // 2, 1)

    def halo_copy(sweep, kind, chunk, a):
        source_at, target_at, to = (
            ((0, 0), (1, 0), partner),
            ((0, 0), (2, 0), outer),
            ((0, 0), (0, 1), ahead),
            ((0, 0), (0, 2), behind),
            ((2, 0), (2, 1), ahead),
            ((2, 0), (2, 2), behind),
            ((0, 1), (1, 1), partner),
            ((0, 2), (1, 2), partner),
        )[kind]
        at = lambda place: exts[sweep][chunk].at[place[0] * 3 + place[1], a]
        group = chunk * SIDE + a
        return pltpu.make_async_remote_copy(
            src_ref=at(source_at), dst_ref=at(target_at),
            send_sem=halo_send.at[sweep, kind, group], recv_sem=halo_recv.at[sweep, kind, group],
            device_id=to, device_id_type=MESH)

    def send_own(sweep, chunk, a):
        for kind in (1, 2, 3, 0):
            halo_copy(sweep, kind, chunk, a).start()

    def over_rows(body):
        def step(a, carry):
            body(a)
            return carry
        lax.fori_loop(0, SIDE, step, 0)

    def pass_across(sweep, chunk):
        def body(a):
            halo_copy(sweep, 1, chunk, a).wait_recv()
            halo_copy(sweep, 4, chunk, a).start()
            halo_copy(sweep, 5, chunk, a).start()
        over_rows(body)

    def pass_partner(sweep, chunk):
        def body(a):
            halo_copy(sweep, 2, chunk, a).wait_recv()
            halo_copy(sweep, 6, chunk, a).start()
            halo_copy(sweep, 3, chunk, a).wait_recv()
            halo_copy(sweep, 7, chunk, a).start()
        over_rows(body)

    def arrive(sweep, chunk):
        def body(a):
            for kind in (0, 4, 5, 6, 7):
                halo_copy(sweep, kind, chunk, a).wait_recv()
        over_rows(body)

    def transform(chunk):
        def body(a):
            group = chunk * SIDE + a
            in_own(group).wait()
            for step in OTHERS:
                in_copy(group, step).wait_recv()
            steps = recv[group].astype(jnp.int32).astype(jnp.float32).T * own_scales(tm, lambda step: scale_recv[step, group])
            spectrum = jnp.dot(steps, fwd[...],
                               precision=lax.Precision.HIGHEST, preferred_element_type=jnp.float32)
            source[group] = spectrum
            exts[0][chunk][0, a] = apply_inverse(a, spectrum).astype(jnp.bfloat16)
            send_own(0, chunk, a)
        over_rows(body)

    def relaxed(sweep, chunk, a):
        parts = []
        for b in range(SIDE):
            total = jnp.zeros((BLOCK, COLS), jnp.float32)
            for link in range(LINKS):
                up = lax.rem(conn[a, b, 0, link] - 2 * row + 18, 16)
                across = lax.rem(conn[a, b, 1, link] - 2 * blk + 10, 8)
                up_block, across_block = up // 2, across // 2
                row_place = jnp.where(up_block == 1, 0, jnp.where(up_block == 2 - 2 * odd, 1, 2))
                col_place = jnp.where(across_block == 1, 0, jnp.where(across_block == 0, 1, 2))
                named = exts[sweep][chunk][row_place * 3 + col_place, lax.rem(up, 2)]
                product = jnp.dot(stiff[(a * SIDE + b) * LINKS + link], named, preferred_element_type=jnp.float32)
                factor = seg[a, b, link].astype(jnp.float32)
                total = total + product * jnp.where(first_block == (lax.rem(across, 2) == 0), factor, 0.0)
            parts.append(total)
        mine = jnp.where(first_block, parts[0], parts[1])
        other = jnp.where(first_block, parts[1], parts[0])
        other = jnp.where(first_block, pltpu.roll(other, COLS - 1, 1), pltpu.roll(other, 1, 1))
        return apply_inverse(a, source[chunk * SIDE + a] - (mine + other))

    def first_sweep(chunk):
        def body(a):
            exts[1][chunk][0, a] = relaxed(0, chunk, a).astype(jnp.bfloat16)
            send_own(1, chunk, a)
        over_rows(body)

    def out_copy(group, step):
        to = other(tm, step)
        return pltpu.make_async_remote_copy(
            src_ref=result.at[group, rows_of(to)], dst_ref=landed.at[group, rows_of(tm)],
            send_sem=out_send.at[group, step], recv_sem=out_recv.at[group, step],
            device_id={"tm": to}, device_id_type=MESH)

    def out_scale(group, step):
        return pltpu.make_async_remote_copy(
            src_ref=scale_result.at[group], dst_ref=scale_landed.at[group, tm],
            send_sem=out_scale_send.at[group, step], recv_sem=out_scale_recv.at[group, step],
            device_id={"tm": other(tm, step)}, device_id_type=MESH)

    def out_own(group):
        return pltpu.make_async_copy(result.at[group, rows_of(tm)], landed.at[group, rows_of(tm)], own_sem.at[group])

    def own_scale(group):
        return pltpu.make_async_copy(scale_result.at[group], scale_landed.at[group, tm], own_scale_sem.at[group])

    def second_sweep(chunk):
        def body(a):
            group = chunk * SIDE + a
            signal = lax.dot_general(bwd[...], relaxed(1, chunk, a), (((1,), (1,)), ((), ())),
                                     precision=lax.Precision.HIGHEST, preferred_element_type=jnp.float32)
            result[group], scale_result[group] = encode(signal)
            own_scale(group).start()
            for step in OTHERS:
                out_scale(group, step).start()
                out_copy(group, step).start()
            out_own(group).start()
        over_rows(body)

    def final_copy(chunk, a):
        return pltpu.make_async_copy(
            final.at[:, :, chunk, :, a], out.at[:, :, chunk, :, a], final_sem.at[chunk * SIDE + a])

    def finish(chunk):
        def body(a):
            group = chunk * SIDE + a
            out_own(group).wait()
            own_scale(group).wait()
            for step in OTHERS:
                out_copy(group, step).wait_recv()
                out_scale(group, step).wait_recv()
            scales = own_scales(tm, lambda step: scale_landed[group, step])
            scales = jnp.broadcast_to(scales, (COLS, COLS)).T
            value = landed[group].astype(jnp.int32).astype(jnp.float32) * jnp.concatenate(
                [scales] * (BLOCK // COLS), axis=1)
            for step in range(TM):
                part = value[step * ROWS:(step + 1) * ROWS]
                final[:, step, chunk, :, a] = part.reshape(OWN_STEPS, PAIR, SIDE, BLOCK)
            final_copy(chunk, a).start()
        over_rows(body)

    for step in OTHERS:
        scale_copy(step).wait_recv()
    transform(0)
    transform(1)
    pass_across(0, 0)
    pass_partner(0, 0)
    pass_across(0, 1)
    arrive(0, 0)
    for load in loads[6:]:
        load.wait()
    first_sweep(0)
    pass_partner(0, 1)
    pass_across(1, 0)
    arrive(0, 1)
    first_sweep(1)
    pass_partner(1, 0)
    pass_across(1, 1)
    arrive(1, 0)
    second_sweep(0)
    pass_partner(1, 1)
    arrive(1, 1)
    second_sweep(1)
    finish(0)
    finish(1)

    def drain(group, carry):
        for step in OTHERS:
            in_copy(group, step).wait_send()
            out_copy(group, step).wait_send()
            out_scale(group, step).wait_send()
        final_copy(group // SIDE, lax.rem(group, SIDE)).wait()
        return carry

    for step in OTHERS:
        scale_copy(step).wait_send()
    lax.fori_loop(0, GROUPS, drain, 0)
    for sweep in range(2):
        for chunk in range(CHUNKS):
            over_rows(lambda a: [halo_copy(sweep, kind, chunk, a).wait_send() for kind in range(8)])


def shards(right_side, stiffness, segments, connectivity, lumped_mass, stiff_diag):
    hbm = pl.BlockSpec(memory_space=pltpu.HBM)
    dma = pltpu.SemaphoreType.DMA
    split = (OWN_STEPS, TM, CHUNKS, PAIR, SIDE, SIDE, BLOCK)
    links = jnp.transpose(connectivity, (0, 1, 3, 2))
    ext = pltpu.VMEM((9, SIDE, BLOCK, COLS), jnp.bfloat16)
    rows = pltpu.VMEM((GROUPS, COLS, BLOCK), jnp.int16)
    between = dma((GROUPS, TM))
    decoded = pl.pallas_call(
        kernel,
        out_shape=jax.ShapeDtypeStruct(split, jnp.float32),
        in_specs=[hbm] * 9,
        out_specs=hbm,
        scratch_shapes=[
            pltpu.VMEM((SIDE * SIDE * LINKS, BLOCK, BLOCK), jnp.bfloat16),
            pltpu.SMEM(segments.shape, jnp.int32),
            pltpu.SMEM(links.shape, jnp.int32),
            pltpu.VMEM(lumped_mass.shape, jnp.float32),
            pltpu.VMEM(stiff_diag.shape, jnp.float32),
            pltpu.VMEM((COLS, COLS), jnp.float32),
            pltpu.VMEM((COLS, COLS), jnp.float32),
            pltpu.VMEM((8, COLS), jnp.float32),
            pltpu.VMEM(split, jnp.float32),
            rows,
            rows,
            pltpu.VMEM((GROUPS, 1, COLS), jnp.float32),
            pltpu.VMEM((TM, GROUPS, 1, COLS), jnp.float32),
            ext, ext, ext, ext,
            pltpu.VMEM((GROUPS, BLOCK, COLS), jnp.float32),
            pltpu.VMEM((SIDE, BLOCK, COLS), jnp.float32),
            pltpu.VMEM((SIDE, BLOCK, COLS), jnp.float32),
            rows,
            pltpu.VMEM((GROUPS, 1, COLS), jnp.float32),
            rows,
            pltpu.VMEM((GROUPS, TM, 1, COLS), jnp.float32),
            pltpu.VMEM(split, jnp.float32),
            dma((9,)),
            between,
            between,
            dma((GROUPS,)),
            dma((GROUPS,)),
            dma((TM,)),
            dma((TM,)),
            dma((2, 8, GROUPS)),
            dma((2, 8, GROUPS)),
            between,
            between,
            between,
            between,
            dma((GROUPS,)),
        ],
        compiler_params=pltpu.CompilerParams(
            collective_id=0, has_side_effects=True, vmem_limit_bytes=60 * 2**20),
    )(right_side.reshape(split), stiffness.reshape(SIDE * SIDE * LINKS, BLOCK, BLOCK), segments, links,
      lumped_mass, stiff_diag, *tables())
    result = pl.pallas_call(
        copy_kernel,
        out_shape=jax.ShapeDtypeStruct(split, jnp.float32),
        in_specs=[hbm],
        out_specs=hbm,
        scratch_shapes=[pltpu.VMEM(split, jnp.float32), dma((OWN_STEPS,)), dma((OWN_STEPS,))],
        compiler_params=pltpu.CompilerParams(vmem_limit_bytes=60 * 2**20),
    )(decoded)
    return result.reshape(right_side.shape)


def solution(mesh):
    placed = (
        P("tm", None, "row", "blk", None),
        P("row", "blk", None, None, None),
        P("row", "blk", None),
        P("row", "blk", None, None),
        P("row", "blk", None),
        P("row", "blk", None),
    )
    return jax.shard_map(
        shards,
        mesh=mesh,
        in_specs=placed,
        out_specs=P("tm", None, "row", "blk", None),
        check_vma=False,
    )
```

```python
import math

import jax
import jax.numpy as jnp
import numpy as np
from jax import lax
from jax.experimental import pallas as pl
from jax.experimental.pallas import tpu as pltpu
from jax.sharding import PartitionSpec as P

MESH = pl.DeviceIdType.MESH
STEPS = 32
BLOCK = 384
LINKS = 10
CASES = 32
SIDE = 2
CHUNKS = 2
GROUPS = CHUNKS * SIDE
TM = 8
ALPHA = 0.5
OWN_STEPS = STEPS // TM
OWN_CASES = CASES // TM
PAIR = OWN_CASES // CHUNKS
ROWS = OWN_STEPS * PAIR * SIDE
COLS = STEPS * PAIR * SIDE


def tables():
    rate = math.log(ALPHA) / STEPS
    root = ALPHA ** (1.0 / STEPS)
    n = np.arange(STEPS)
    k = np.arange(STEPS // 2)
    angle = 2.0 * np.pi / STEPS * ((n[:, None] * k[None, :]) % STEPS)
    real, imag = np.cos(angle), -np.sin(angle)
    alternate = np.where(n % 2 == 0, 1.0, -1.0)
    imag[:, 0] = alternate
    forward = np.concatenate([real, imag], axis=1) * np.exp(n * rate)[:, None]
    back_real, back_imag = 2.0 * np.cos(angle), -2.0 * np.sin(angle)
    back_real[:, 0] = 1.0
    back_imag[:, 0] = alternate
    backward = np.concatenate([back_real, back_imag], axis=1) / STEPS * np.exp(-n * rate)[:, None]
    eye = np.eye(PAIR * SIDE)
    theta = 2.0 * np.pi * k / STEPS
    shift_re = np.concatenate([1.0 - root * np.cos(theta)] * 2)
    shift_re[STEPS // 2] = 1.0 + root
    shift_im = np.concatenate([root * np.sin(theta), -root * np.sin(theta)])
    shift_im[0] = shift_im[STEPS // 2] = 0.0
    shifts = np.zeros((8, COLS))
    shifts[0] = np.repeat(shift_re, PAIR * SIDE)
    shifts[1] = np.repeat(shift_im, PAIR * SIDE)
    as_f32 = lambda a: np.asarray(a, np.float32)
    return as_f32(np.kron(forward, eye)), as_f32(np.kron(backward, eye)), as_f32(shifts)


def own_scales(tm, row_from):
    lane = lax.broadcasted_iota(jnp.int32, (1, COLS), 1)
    scales = jnp.zeros((1, COLS), jnp.float32)
    for step in range(TM):
        moved = pltpu.roll(row_from(step), lax.rem((step - tm + TM) * ROWS, COLS), 1)
        scales = jnp.where(lane // ROWS == step, moved, scales)
    return scales


OTHERS = range(1, TM)


def other(tm, step):
    half, place = tm // 4, lax.rem(tm, 4)
    return lax.rem(half + (step <= 4), 2) * 4 + lax.rem(place + (step if step <= 4 else step - 4), 4)


def kernel(right, stiff_hbm, seg_hbm, conn_hbm, mass_hbm, diag_hbm, fwd_hbm, bwd_hbm, shifts_hbm, out,
           stiff, seg, conn, mass, diag, fwd, bwd, shifts, given, coded, recv, scale_given, scale_recv,
           ext00, ext01, ext10, ext11, source, coef_a, coef_b,
           result, scale_result, landed, scale_landed,
           load_sem, in_send, in_recv, own_sem, own_scale_sem, scale_send, scale_sem, halo_send, halo_recv,
           out_send, out_recv, out_scale_send, out_scale_recv):
    tm, row, blk = lax.axis_index("tm"), lax.axis_index("row"), lax.axis_index("blk")
    odd = lax.rem(row, 2)
    partner = {"row": row + 1 - 2 * odd}
    outer = {"row": lax.rem(row + 7 + 2 * odd, 8)}
    ahead = {"blk": lax.rem(blk + 1, 4)}
    behind = {"blk": lax.rem(blk + 3, 4)}
    exts = ((ext00, ext01), (ext10, ext11))

    barrier = pltpu.get_barrier_semaphore()
    for step in OTHERS:
        pl.semaphore_signal(barrier, inc=1, device_id={"tm": other(tm, step)}, device_id_type=MESH)
    for near in (partner, outer, ahead, behind):
        pl.semaphore_signal(barrier, inc=1, device_id=near, device_id_type=MESH)

    loads = [
        pltpu.make_async_copy(source_ref, target_ref, load_sem.at[place])
        for place, (source_ref, target_ref) in enumerate((
            (right, given), (mass_hbm, mass), (diag_hbm, diag), (shifts_hbm, shifts), (fwd_hbm, fwd), (bwd_hbm, bwd),
            (seg_hbm, seg), (conn_hbm, conn), (stiff_hbm, stiff)))
    ]
    for load in loads:
        load.start()

    lane = lax.broadcasted_iota(jnp.int32, (1, COLS), 1)

    def encode(value):
        largest = jnp.maximum(jnp.max(jnp.abs(value), axis=1, keepdims=True), 1e-30)
        whole = jnp.round(value * (32767.0 / largest)).astype(jnp.int32).astype(jnp.int16)
        scales = jnp.broadcast_to(largest * (1.0 / 32767.0), (COLS, COLS)).T
        return whole, scales[0:1, :]

    loads[0].wait()

    def code(group, carry):
        chunk, a = group // SIDE, lax.rem(group, SIDE)
        value = jnp.concatenate([given[:, to, chunk, :, a].reshape(ROWS, BLOCK) for to in range(TM)], axis=0)
        coded[group], scale_given[group] = encode(value)
        return carry

    lax.fori_loop(0, GROUPS, code, 0)
    scale_recv[tm] = scale_given[...]
    pl.semaphore_wait(barrier, TM - 1 + 4)

    def scale_copy(step):
        return pltpu.make_async_remote_copy(
            src_ref=scale_given, dst_ref=scale_recv.at[tm], send_sem=scale_send.at[step], recv_sem=scale_sem.at[step],
            device_id={"tm": other(tm, step)}, device_id_type=MESH)

    def rows_of(owner):
        return pl.ds(pl.multiple_of(owner * ROWS, ROWS), ROWS)

    def in_copy(group, step):
        to = other(tm, step)
        return pltpu.make_async_remote_copy(
            src_ref=coded.at[group, rows_of(to)], dst_ref=recv.at[group, rows_of(tm)],
            send_sem=in_send.at[group, step], recv_sem=in_recv.at[group, step],
            device_id={"tm": to}, device_id_type=MESH)

    def in_own(group):
        return pltpu.make_async_copy(coded.at[group, rows_of(tm)], recv.at[group, rows_of(tm)], own_sem.at[group])

    def start_in(group, carry):
        in_own(group).start()
        for step in OTHERS:
            in_copy(group, step).start()
        return carry

    for step in OTHERS:
        scale_copy(step).start()
    lax.fori_loop(0, GROUPS, start_in, 0)

    first_block = lax.rem(lane, 2) == 0
    for load in loads[1:4]:
        load.wait()

    def by_column(ref, lattice_row):
        column = lambda b: jnp.broadcast_to(ref[lattice_row, b:b + 1, :], (COLS, BLOCK)).T
        return jnp.where(first_block, column(0), column(1))

    for a in range(SIDE):
        mass_t, diag_t = by_column(mass, a), by_column(diag, a)
        diag_re = shifts[0:1, :] * mass_t + diag_t
        diag_im = shifts[1:2, :] * mass_t
        modulus = diag_re * diag_re + diag_im * diag_im
        coef_a[a] = diag_re / modulus
        coef_b[a] = diag_im / modulus
    for load in loads[4:6]:
        load.wait()

    def apply_inverse(a, update):
        return coef_a[a] * update + coef_b[a] * pltpu.roll(update, COLS // 2, 1)

    def halo_copy(sweep, kind, chunk, a):
        source_at, target_at, to = (
            ((0, 0), (1, 0), partner),
            ((0, 0), (2, 0), outer),
            ((0, 0), (0, 1), ahead),
            ((0, 0), (0, 2), behind),
            ((2, 0), (2, 1), ahead),
            ((2, 0), (2, 2), behind),
            ((0, 1), (1, 1), partner),
            ((0, 2), (1, 2), partner),
        )[kind]
        at = lambda place: exts[sweep][chunk].at[place[0] * 3 + place[1], a]
        group = chunk * SIDE + a
        return pltpu.make_async_remote_copy(
            src_ref=at(source_at), dst_ref=at(target_at),
            send_sem=halo_send.at[sweep, kind, group], recv_sem=halo_recv.at[sweep, kind, group],
            device_id=to, device_id_type=MESH)

    def send_own(sweep, chunk, a):
        for kind in (1, 2, 3, 0):
            halo_copy(sweep, kind, chunk, a).start()

    def over_rows(body):
        def step(a, carry):
            body(a)
            return carry
        lax.fori_loop(0, SIDE, step, 0)

    def pass_across(sweep, chunk):
        def body(a):
            halo_copy(sweep, 1, chunk, a).wait_recv()
            halo_copy(sweep, 4, chunk, a).start()
            halo_copy(sweep, 5, chunk, a).start()
        over_rows(body)

    def pass_partner(sweep, chunk):
        def body(a):
            halo_copy(sweep, 2, chunk, a).wait_recv()
            halo_copy(sweep, 6, chunk, a).start()
            halo_copy(sweep, 3, chunk, a).wait_recv()
            halo_copy(sweep, 7, chunk, a).start()
        over_rows(body)

    def arrive(sweep, chunk):
        def body(a):
            for kind in (0, 4, 5, 6, 7):
                halo_copy(sweep, kind, chunk, a).wait_recv()
        over_rows(body)

    def transform(chunk):
        def body(a):
            group = chunk * SIDE + a
            in_own(group).wait()
            for step in OTHERS:
                in_copy(group, step).wait_recv()
            steps = recv[group].astype(jnp.int32).astype(jnp.float32).T * own_scales(tm, lambda step: scale_recv[step, group])
            spectrum = jnp.dot(steps, fwd[...],
                               precision=lax.Precision.HIGHEST, preferred_element_type=jnp.float32)
            source[group] = spectrum
            exts[0][chunk][0, a] = apply_inverse(a, spectrum).astype(jnp.bfloat16)
            send_own(0, chunk, a)
        over_rows(body)

    def relaxed(sweep, chunk, a):
        parts = []
        for b in range(SIDE):
            total = jnp.zeros((BLOCK, COLS), jnp.float32)
            for link in range(LINKS):
                up = lax.rem(conn[a, b, 0, link] - 2 * row + 18, 16)
                across = lax.rem(conn[a, b, 1, link] - 2 * blk + 10, 8)
                up_block, across_block = up // 2, across // 2
                row_place = jnp.where(up_block == 1, 0, jnp.where(up_block == 2 - 2 * odd, 1, 2))
                col_place = jnp.where(across_block == 1, 0, jnp.where(across_block == 0, 1, 2))
                named = exts[sweep][chunk][row_place * 3 + col_place, lax.rem(up, 2)]
                product = jnp.dot(stiff[(a * SIDE + b) * LINKS + link], named, preferred_element_type=jnp.float32)
                factor = seg[a, b, link].astype(jnp.float32)
                total = total + product * jnp.where(first_block == (lax.rem(across, 2) == 0), factor, 0.0)
            parts.append(total)
        mine = jnp.where(first_block, parts[0], parts[1])
        other = jnp.where(first_block, parts[1], parts[0])
        other = jnp.where(first_block, pltpu.roll(other, COLS - 1, 1), pltpu.roll(other, 1, 1))
        return apply_inverse(a, source[chunk * SIDE + a] - (mine + other))

    def first_sweep(chunk):
        def body(a):
            exts[1][chunk][0, a] = relaxed(0, chunk, a).astype(jnp.bfloat16)
            send_own(1, chunk, a)
        over_rows(body)

    def out_copy(group, step):
        to = other(tm, step)
        return pltpu.make_async_remote_copy(
            src_ref=result.at[group, rows_of(to)], dst_ref=landed.at[group, rows_of(tm)],
            send_sem=out_send.at[group, step], recv_sem=out_recv.at[group, step],
            device_id={"tm": to}, device_id_type=MESH)

    def out_scale(group, step):
        return pltpu.make_async_remote_copy(
            src_ref=scale_result.at[group], dst_ref=scale_landed.at[group, tm],
            send_sem=out_scale_send.at[group, step], recv_sem=out_scale_recv.at[group, step],
            device_id={"tm": other(tm, step)}, device_id_type=MESH)

    def out_own(group):
        return pltpu.make_async_copy(result.at[group, rows_of(tm)], landed.at[group, rows_of(tm)], own_sem.at[group])

    def own_scale(group):
        return pltpu.make_async_copy(scale_result.at[group], scale_landed.at[group, tm], own_scale_sem.at[group])

    def second_sweep(chunk):
        def body(a):
            group = chunk * SIDE + a
            signal = lax.dot_general(bwd[...], relaxed(1, chunk, a), (((1,), (1,)), ((), ())),
                                     precision=lax.Precision.HIGHEST, preferred_element_type=jnp.float32)
            result[group], scale_result[group] = encode(signal)
            own_scale(group).start()
            for step in OTHERS:
                out_scale(group, step).start()
                out_copy(group, step).start()
            out_own(group).start()
        over_rows(body)

    def finish(chunk):
        def body(a):
            group = chunk * SIDE + a
            out_own(group).wait()
            own_scale(group).wait()
            for step in OTHERS:
                out_copy(group, step).wait_recv()
                out_scale(group, step).wait_recv()
            scales = own_scales(tm, lambda step: scale_landed[group, step])
            scales = jnp.broadcast_to(scales, (COLS, COLS)).T
            value = landed[group].astype(jnp.int32).astype(jnp.float32) * jnp.concatenate(
                [scales] * (BLOCK // COLS), axis=1)
            for step in range(TM):
                part = value[step * ROWS:(step + 1) * ROWS]
                out[:, step, chunk, :, a] = part.reshape(OWN_STEPS, PAIR, SIDE, BLOCK)
        over_rows(body)

    for step in OTHERS:
        scale_copy(step).wait_recv()
    def sent_in():
        def body(group, carry):
            for step in OTHERS:
                in_copy(group, step).wait_send()
            return carry
        for step in OTHERS:
            scale_copy(step).wait_send()
        lax.fori_loop(0, GROUPS, body, 0)

    def sent_halo(sweep, chunk):
        over_rows(lambda a: [halo_copy(sweep, kind, chunk, a).wait_send() for kind in range(8)])

    def sent_out(chunk):
        def body(a):
            for step in OTHERS:
                out_copy(chunk * SIDE + a, step).wait_send()
                out_scale(chunk * SIDE + a, step).wait_send()
        over_rows(body)

    transform(0)
    transform(1)
    pass_across(0, 0)
    pass_partner(0, 0)
    pass_across(0, 1)
    arrive(0, 0)
    for load in loads[6:]:
        load.wait()
    first_sweep(0)
    pass_partner(0, 1)
    pass_across(1, 0)
    arrive(0, 1)
    first_sweep(1)
    pass_partner(1, 0)
    sent_in()
    sent_halo(0, 0)
    pass_across(1, 1)
    sent_halo(0, 1)
    arrive(1, 0)
    second_sweep(0)
    pass_partner(1, 1)
    sent_halo(1, 0)
    arrive(1, 1)
    second_sweep(1)
    sent_halo(1, 1)
    finish(0)
    sent_out(0)
    finish(1)
    sent_out(1)


def shards(right_side, stiffness, segments, connectivity, lumped_mass, stiff_diag):
    hbm = pl.BlockSpec(memory_space=pltpu.HBM)
    dma = pltpu.SemaphoreType.DMA
    split = (OWN_STEPS, TM, CHUNKS, PAIR, SIDE, SIDE, BLOCK)
    links = jnp.transpose(connectivity, (0, 1, 3, 2))
    ext = pltpu.VMEM((9, SIDE, BLOCK, COLS), jnp.bfloat16)
    rows = pltpu.VMEM((GROUPS, COLS, BLOCK), jnp.int16)
    between = dma((GROUPS, TM))
    decoded = pl.pallas_call(
        kernel,
        out_shape=pltpu.VMEM(split, jnp.float32),
        in_specs=[hbm] * 9,
        out_specs=pl.BlockSpec(memory_space=pltpu.VMEM),
        scratch_shapes=[
            pltpu.VMEM((SIDE * SIDE * LINKS, BLOCK, BLOCK), jnp.bfloat16),
            pltpu.SMEM(segments.shape, jnp.int32),
            pltpu.SMEM(links.shape, jnp.int32),
            pltpu.VMEM(lumped_mass.shape, jnp.float32),
            pltpu.VMEM(stiff_diag.shape, jnp.float32),
            pltpu.VMEM((COLS, COLS), jnp.float32),
            pltpu.VMEM((COLS, COLS), jnp.float32),
            pltpu.VMEM((8, COLS), jnp.float32),
            pltpu.VMEM(split, jnp.float32),
            rows,
            rows,
            pltpu.VMEM((GROUPS, 1, COLS), jnp.float32),
            pltpu.VMEM((TM, GROUPS, 1, COLS), jnp.float32),
            ext, ext, ext, ext,
            pltpu.VMEM((GROUPS, BLOCK, COLS), jnp.float32),
            pltpu.VMEM((SIDE, BLOCK, COLS), jnp.float32),
            pltpu.VMEM((SIDE, BLOCK, COLS), jnp.float32),
            rows,
            pltpu.VMEM((GROUPS, 1, COLS), jnp.float32),
            rows,
            pltpu.VMEM((GROUPS, TM, 1, COLS), jnp.float32),
            dma((9,)),
            between,
            between,
            dma((GROUPS,)),
            dma((GROUPS,)),
            dma((TM,)),
            dma((TM,)),
            dma((2, 8, GROUPS)),
            dma((2, 8, GROUPS)),
            between,
            between,
            between,
            between,
        ],
        compiler_params=pltpu.CompilerParams(
            collective_id=0, has_side_effects=True, vmem_limit_bytes=56 * 2**20),
    )(right_side.reshape(split), stiffness.reshape(SIDE * SIDE * LINKS, BLOCK, BLOCK), segments, links,
      lumped_mass, stiff_diag, *tables())
    return decoded.reshape(right_side.shape)


def solution(mesh):
    placed = (
        P("tm", None, "row", "blk", None),
        P("row", "blk", None, None, None),
        P("row", "blk", None),
        P("row", "blk", None, None),
        P("row", "blk", None),
        P("row", "blk", None),
    )
    return jax.shard_map(
        shards,
        mesh=mesh,
        in_specs=placed,
        out_specs=P("tm", None, "row", "blk", None),
        check_vma=False,
    )
```
